256 devices in a mesh: group: 32 (over y_hi, z, core), shard: 4 (over x), tensor: 2 (over y_lo).
Axes of the slice: x: 4, y: 4 (y_hi: 2, y_lo: 2; y = y_hi * 2 + y_lo), z: 8, core: 2. Of those that a mesh axis runs over, the one named last changes fastest.
Arguments:
- partials: bfloat16 [12288, 2, 16384], P('group', 'tensor', 'shard'), may hold values from -10 to 10
- index_map: int32 [128, 4], replicated, may hold values from 0 to 31
- sign_bits: int32 [16384], replicated, may hold values from 0 to 1
- blocks: bfloat16 [4, 128, 128], replicated, may hold values from -0.125 to 0.125
Outputs:
- sketch: bfloat16 [12288, 4096], P(('group', 'shard', 'tensor'))
- kernel: float32 [32, 384, 12288], P(None, ('shard', 'tensor'), 'group')
The draws below stay inside these ranges and needn't reach their ends.
All inputs are finite; a program needn't handle non-finite values.
Results may differ from the reference program's by a relative error of at most 0.014.
Values may be sent and summed in bfloat16 or wider, within the bound.
A program may use at most 128 MiB of HBM per device.

```python
import jax
import jax.numpy as jnp
from jax import lax

EX_G = 384
SKETCH = 4096
BLOCK = 128
FAN = 4
PAR = 16384
EXAMPLES = 12288
N_GROUP = 32
N_TENSOR = 2


def draw_partials(key, part):
    key = jax.random.fold_in(key, 11)
    key_common, key_weight, key_noise = jax.random.split(key, 3)
    common = jax.random.normal(key_common, (1, N_TENSOR, PAR), jnp.float32)
    weight = jax.random.uniform(key_weight, (EXAMPLES, 1, 1), jnp.float32, -0.8, 0.8)
    noise_part = jax.random.normal(key_noise, (EXAMPLES, N_TENSOR, PAR), jnp.float32)
    result = noise_part + weight * common
    return jnp.clip(result, -10.0, 10.0).astype(jnp.bfloat16)


def place_ends(array, own_key, low, top_value):
    longest = array.shape.index(max(array.shape))
    spots = []
    for shift in (0, 1):
        where = [jax.random.randint(jax.random.fold_in(own_key, axis), (), 0, length) for axis, length in enumerate(array.shape)]
        where[longest] = (where[longest] + shift) % array.shape[longest]
        spots.append(tuple(where))
    return array.at[spots[0]].set(low).at[spots[1]].set(top_value)


def bell_draw(rng, shape, spread, reach, kind=jnp.bfloat16):
    entries = spread * jax.random.normal(rng, shape, jnp.float32)
    return jnp.clip(entries, min=-reach, max=reach).astype(kind)


def setup_inputs(seed: int = 0) -> dict:
    streams_of = jax.random.split(jax.random.key(seed), 5)
    partials = draw_partials(jax.random.fold_in(streams_of[4], 71), 0)
    index_map = place_ends(jax.random.randint(streams_of[1], (PAR // BLOCK, FAN), 0, SKETCH // BLOCK), jax.random.fold_in(streams_of[1], 1), 0, (SKETCH // BLOCK) - 1).astype(jnp.int32)
    sign_bits = place_ends(jax.random.randint(streams_of[2], (PAR,), 0, 2), jax.random.fold_in(streams_of[2], 1), 0, 1).astype(jnp.int32)
    blocks = bell_draw(streams_of[3], (FAN, BLOCK, BLOCK), (BLOCK * PAR * FAN // SKETCH) ** -0.5, 0.125)
    return {"partials": partials, "index_map": index_map, "sign_bits": sign_bits, "blocks": blocks}


def reference(partials, index_map, sign_bits, blocks):
    block_count = PAR // BLOCK
    sketch_blocks = SKETCH // BLOCK
    sign_rows = (2 * sign_bits - 1).astype(jnp.float32).reshape(block_count, BLOCK)
    onehot = (index_map[:, :, None] == jnp.arange(sketch_blocks, dtype=jnp.int32)[None, None, :]).astype(jnp.float32)
    dense_blocks = blocks.astype(jnp.float32)

    def sketch_group(group_part):
        gradient = jnp.sum(group_part.astype(jnp.float32), axis=1)
        signed = gradient.reshape(EX_G, block_count, BLOCK) * sign_rows[None]
        projected = jnp.einsum("ebc,jcd->ebjd", signed, dense_blocks, precision=lax.Precision.HIGHEST)
        summed = jnp.einsum("ebjd,bjs->esd", projected, onehot, precision=lax.Precision.HIGHEST)
        return summed.reshape(EX_G, SKETCH)

    sketch_sums = lax.map(sketch_group, partials.reshape(N_GROUP, EX_G, N_TENSOR, PAR))
    sketch = sketch_sums.reshape(EXAMPLES, SKETCH).astype(jnp.bfloat16)

    def kernel_group(group_rows):
        return jnp.dot(group_rows, sketch.T, preferred_element_type=jnp.float32) / SKETCH

    kernel = lax.map(kernel_group, sketch.reshape(N_GROUP, EX_G, SKETCH))
    return sketch, kernel
```

```python
import functools

import jax
import jax.numpy as jnp
from jax import lax
from jax.experimental import pallas as pl
from jax.experimental.pallas import tpu as pltpu
from jax.sharding import PartitionSpec as P

SKETCH = 4096
BLOCK = 128
FAN = 4
SB = SKETCH // BLOCK
NX, NT, NZ, NY, NC = 4, 2, 8, 2, 2
PART = 3
ROWS = 16
MESH = pl.DeviceIdType.MESH
F32 = jnp.float32
BF16 = jnp.bfloat16


def split_pair(values):
    upper = values.astype(BF16)
    return upper, (values - upper.astype(F32)).astype(BF16)


def kernel_body(
    x_ref, map_ref, sign_ref, blocks_ref, sketch_ref, out_ref,
    rx, gath, rows, grad, wide, low, onehot, signs, stacked,
    local_sem, a2a_s, a2a_r, sib_s, sib_r, y2_s, y2_r, yp_s, yp_r, x_s, x_r, z_s, z_r,
):
    group = lax.axis_index("group")
    x = lax.axis_index("shard")
    t = lax.axis_index("tensor")
    yh = group // (NZ * NC)
    z = lax.rem(group, NZ * NC) // NC
    c = lax.rem(group, NC)
    d = x * NT + t

    def at_group(yy, zz, cc):
        return {"group": (yy * NZ + zz) * NC + cc}

    sibling = at_group(yh, z, 1 - c)
    across = at_group(1 - yh, z, c)
    ahead = at_group(yh, lax.rem(z + 1, NZ), c)
    behind = at_group(yh, lax.rem(z + NZ - 1, NZ), c)
    z_way = (ahead, behind)

    def member(j):
        e = lax.rem(d + j, NX * NT)
        return e, {"shard": e // NT, "tensor": lax.rem(e, NT)}

    barrier = pltpu.get_barrier_semaphore()
    for target in [member(j)[1] for j in range(1, 8)] + [sibling, across, ahead, behind]:
        pl.semaphore_signal(barrier, inc=1, device_id=target, device_id_type=MESH)
    pl.semaphore_wait(barrier, 11)

    def remote(src, dst, s, r, target):
        return pltpu.make_async_remote_copy(
            src_ref=src, dst_ref=dst, send_sem=s, recv_sem=r, device_id=target, device_id_type=MESH
        )

    started = []

    def start(copy):
        copy.start()
        started.append(copy)
        return copy

    def exchange(i):
        own = pltpu.make_async_copy(
            x_ref.at[pl.ds(pl.multiple_of(d * PART * ROWS + i * ROWS, ROWS), ROWS), :],
            rx.at[i, x, t], local_sem.at[i],
        )
        own.start()
        copies = []
        for j in range(1, 8):
            e, target = member(j)
            src = x_ref.at[pl.ds(pl.multiple_of(e * PART * ROWS + i * ROWS, ROWS), ROWS), :]
            copies.append(start(remote(src, rx.at[i, x, t], a2a_s.at[i, j - 1], a2a_r.at[i, j - 1], target)))
        return own, copies

    def project(i):
        @pl.loop(0, NX)
        def _(xx):
            for b in range(SB):
                lanes = pl.ds(b * BLOCK, BLOCK)
                both = rx[i, xx, 0, :, lanes].astype(F32) + rx[i, xx, 1, :, lanes].astype(F32)
                grad[pl.ds(xx * SB + b, ROWS, stride=NX * SB), :] = both

        @pl.loop(0, ROWS // 2)
        def _(pair):
            parts = []
            for e in range(2):
                signed = grad[pl.ds(pl.multiple_of((pair * 2 + e) * BLOCK, BLOCK), BLOCK), :] * signs[...]
                upper, lower = split_pair(signed)
                parts.append(jnp.concatenate([upper, lower], axis=0))
            summed = jnp.dot(onehot[...], jnp.concatenate(parts, axis=1), preferred_element_type=F32)
            upper, lower = split_pair(summed)
            for e in range(2):
                place = pl.ds(pl.multiple_of((pair * 2 + e) * SB, SB), SB)
                cols = slice(e * BLOCK, (e + 1) * BLOCK)
                for f in range(FAN):
                    fr = slice(f * SB, (f + 1) * SB)
                    wide[place, f * BLOCK:(f + 1) * BLOCK] = upper[fr, cols]
                    wide[place, (FAN + f) * BLOCK:(FAN + f + 1) * BLOCK] = lower[fr, cols]

        low[...] = jnp.dot(wide[...], stacked[...], preferred_element_type=F32)
        for s in range(SB):
            piece = low[pl.ds(s, ROWS, stride=SB), :].astype(BF16)
            lanes = slice(s * BLOCK, (s + 1) * BLOCK)
            gath[z, c, yh, i, :, lanes] = piece
            rows[x, t, i, :, lanes] = piece
            sketch_ref[i * ROWS:(i + 1) * ROWS, lanes] = piece

    def spread(i):
        own = gath.at[z, c, yh, i]
        zc = [start(remote(own, own, z_s.at[i, w, 0], z_r.at[i, w, 0], z_way[w])) for w in range(2)]
        y2 = start(remote(own, own, y2_s.at[i], y2_r.at[i], across))
        mine = rows.at[x, t, i]
        yp = start(remote(mine, mine, yp_s.at[i], yp_r.at[i], {"tensor": 1 - t}))
        sb = start(remote(own, own, sib_s.at[i, 0], sib_r.at[i, 0], sibling))
        return zc, y2, yp, sb

    def along_x(i, k, tt):
        block = rows.at[x, tt, i]
        return [
            start(remote(block, block, x_s.at[i, k, j - 1], x_r.at[i, k, j - 1], {"shard": lax.rem(x + j, NX)}))
            for j in (1, 3, 2)
        ]

    def relay_across(i):
        other = gath.at[z, c, 1 - yh, i]
        zc = [start(remote(other, other, z_s.at[i, w, 1], z_r.at[i, w, 1], z_way[w])) for w in range(2)]
        sb = start(remote(other, other, sib_s.at[i, 1], sib_r.at[i, 1], sibling))
        return zc, sb

    def z_block(w, h, i, both, k=None):
        zz = lax.rem(z + NZ - h, NZ) if w == 0 else lax.rem(z + h, NZ)
        return gath.at[zz, c, :, i] if both else gath.at[zz, c, k, i]

    def z_step(i, h, arriving):
        out, sbs = [], []
        for w in range(2):
            for copy in arriving[w]:
                copy.wait_recv()
            if h < 3:
                block = z_block(w, h, i, True)
                out.append([start(remote(block, block, z_s.at[i, w, h + 1], z_r.at[i, w, h + 1], z_way[w]))])
            elif h == 3:
                block = z_block(w, h, i, False, yh if w == 0 else 1 - yh)
                out.append([start(remote(block, block, z_s.at[i, w, 4], z_r.at[i, w, 4], z_way[w]))])
            block = z_block(w, h, i, True) if h < 4 else z_block(w, h, i, False, yh if w == 0 else 1 - yh)
            sbs.append(start(remote(block, block, sib_s.at[i, 1 + w * 4 + h], sib_r.at[i, 1 + w * 4 + h], sibling)))
        return out, sbs

    exchanges = [exchange(0)]

    targets = lax.broadcasted_iota(jnp.int32, (SB, BLOCK), 0)
    for f in range(FAN):
        hot = jnp.where(map_ref[f:f + 1, :] == targets, 1.0, 0.0).astype(BF16)
        onehot[f * SB:(f + 1) * SB, :BLOCK] = hot
        onehot[f * SB:(f + 1) * SB, BLOCK:] = hot
    signs[...] = (2 * sign_ref[...] - 1).astype(F32)
    for f in range(FAN):
        stacked[f * BLOCK:(f + 1) * BLOCK, :] = blocks_ref[f]
        stacked[(FAN + f) * BLOCK:(FAN + f + 1) * BLOCK, :] = blocks_ref[f]

    arrive_z = {}
    arrive_row = []
    arrive_sib = []

    def first(i):
        own, copies = exchanges[i]
        own.wait()
        for copy in copies:
            copy.wait_recv()
        if i + 1 < PART:
            exchanges.append(exchange(i + 1))
        project(i)
        zc, y2, yp, sb = spread(i)
        arrive_row.extend(along_x(i, 0, t))
        y2.wait_recv()
        zc2, sb2 = relay_across(i)
        yp.wait_recv()
        arrive_row.extend(along_x(i, 1, 1 - t))
        arrive_sib.extend([sb, sb2])
        arrive_z[i, 1] = [[zc[w], zc2[w]] for w in range(2)]

    def hop(i, h):
        out, sbs = z_step(i, h, arrive_z[i, h])
        arrive_sib.extend(sbs)
        if out:
            arrive_z[i, h + 1] = out

    first(0)
    hop(0, 1)
    hop(0, 2)
    first(1)
    hop(0, 3)
    hop(1, 1)
    hop(0, 4)
    hop(1, 2)
    first(2)
    hop(1, 3)
    hop(2, 1)
    hop(1, 4)
    hop(2, 2)
    hop(2, 3)
    hop(2, 4)
    for copy in arrive_row:
        copy.wait_recv()
    for copy in arrive_sib:
        copy.wait_recv()

    @pl.loop(0, NZ // 2)
    def _(q):
        left = gath[pl.ds(q * 2, 2)].reshape(2 * NC * NY * PART * ROWS, SKETCH)
        right = rows[...].reshape(NX * NT * PART * ROWS, SKETCH)
        tile = lax.dot_general(left, right, (((1,), (1,)), ((), ())), preferred_element_type=F32) * (1.0 / SKETCH)
        tile = tile.reshape(2, NC, NY, PART * ROWS, NX * NT * PART * ROWS)
        for a in range(2):
            for cc in range(NC):
                for yy in range(NY):
                    out_ref[yy, q * 2 + a, cc] = tile[a, cc, yy]

    for copy in started:
        copy.wait_send()


def on_device(partials, index_map, sign_bits, blocks):
    count = NX * NT * PART * ROWS
    piece = (ROWS, SKETCH)
    dma = pltpu.SemaphoreType.DMA
    vmem = pl.BlockSpec(memory_space=pltpu.VMEM)
    sketch, kernel = pl.pallas_call(
        kernel_body,
        out_shape=(
            jax.ShapeDtypeStruct((PART * ROWS, SKETCH), BF16),
            jax.ShapeDtypeStruct((NY, NZ, NC, PART * ROWS, count), F32),
        ),
        in_specs=[pl.BlockSpec(memory_space=pl.ANY), vmem, vmem, vmem],
        out_specs=(vmem, vmem),
        scratch_shapes=[
            pltpu.VMEM((PART, NX, NT) + piece, BF16),
            pltpu.VMEM((NZ, NC, NY, PART) + piece, BF16),
            pltpu.VMEM((NX, NT, PART) + piece, BF16),
            pltpu.VMEM((ROWS * BLOCK, BLOCK), F32),
            pltpu.VMEM((ROWS * SB, 2 * FAN * BLOCK), BF16),
            pltpu.VMEM((ROWS * SB, BLOCK), F32),
            pltpu.VMEM((FAN * SB, 2 * BLOCK), BF16),
            pltpu.VMEM((BLOCK, BLOCK), F32),
            pltpu.VMEM((2 * FAN * BLOCK, BLOCK), BF16),
            dma((PART,)),
            dma((PART, 7)), dma((PART, 7)),
            dma((PART, 10)), dma((PART, 10)),
            dma((PART,)), dma((PART,)),
            dma((PART,)), dma((PART,)),
            dma((PART, 2, 3)), dma((PART, 2, 3)),
            dma((PART, 2, 5)), dma((PART, 2, 5)),
        ],
        compiler_params=pltpu.CompilerParams(
            collective_id=0, has_side_effects=True, vmem_limit_bytes=56 * 2**20
        ),
        cost_estimate=pl.CostEstimate(flops=6 * 10**9, bytes_accessed=6 * 10**6, transcendentals=0),
        name="sketch_kernel",
    )(
        partials.reshape(count, -1),
        index_map.T,
        sign_bits.reshape(BLOCK, BLOCK),
        blocks,
    )
    return sketch, kernel.reshape(NY * NZ * NC, PART * ROWS, count)


def solution(mesh):
    placed = (P("group", "tensor", "shard"), P(), P(), P())
    return jax.shard_map(
        on_device,
        mesh=mesh,
        in_specs=placed,
        out_specs=(P(("group", "shard", "tensor"), None), P(None, ("shard", "tensor"), "group")),
        check_vma=False,
    )
```

```python
import math

import jax
import jax.numpy as jnp
from jax import lax
from jax.experimental import pallas as pl
from jax.experimental.pallas import tpu as pltpu
from jax.sharding import PartitionSpec as P

SKETCH = 4096
BLOCK = 128
FAN = 4
SB = SKETCH // BLOCK
NX, NT, NZ, NY, NC = 4, 2, 8, 2, 2
PART = 3
ROWS = 16
CUTS = 2
HALF = (True, False, False)
RAW = (False, True, True)
FIRST = 2
ORDER = (
    ('terms', 0, 0), ('terms', 0, 1), ('raw_sketch', 1), ('begin', 2), ('sketch', 0), ('raw_finish', 1),
    ('relay', 0), ('hop', 0, 0, 0, 1), ('hop', 0, 0, 1, 1), ('relay', 1), ('hop', 1, 0, 0, 1), ('hop', 1, 0, 1, 1),
    ('raw_sketch', 2), ('hop', 0, 0, 0, 2), ('hop', 0, 0, 1, 2), ('cross', 0, 0, 1), ('cross', 0, 1, 1),
    ('hop', 1, 1, 0, 1), ('hop', 1, 1, 1, 1), ('hop', 1, 0, 0, 2), ('hop', 1, 0, 1, 2), ('raw_finish', 2),
    ('rows_begin', 0), ('rows_begin', 1), ('rows_begin', 2), ('hop', 0, 0, 0, 3), ('hop', 0, 0, 1, 3),
    ('cross', 0, 0, 2), ('hop', 1, 1, 0, 2), ('hop', 1, 1, 1, 2), ('cross', 0, 1, 2), ('hop', 1, 0, 0, 3),
    ('hop', 1, 0, 1, 3), ('relay', 2), ('hop', 2, 0, 0, 1), ('hop', 2, 0, 1, 1), ('rows_send', 0),
    ('hop', 0, 0, 0, 4), ('hop', 0, 0, 1, 4), ('rows_send', 1), ('hop', 1, 1, 0, 3), ('hop', 1, 1, 1, 3),
    ('rows_send', 2), ('hop', 1, 0, 0, 4), ('hop', 2, 1, 1, 1), ('rows_pass', 0, 0), ('rows_pass', 0, 1),
    ('hop', 2, 1, 0, 1), ('hop', 2, 0, 1, 2), ('cross', 0, 0, 3), ('hop', 2, 0, 0, 2), ('hop', 1, 1, 1, 4),
    ('cross', 0, 1, 3), ('rows_pass', 1, 0), ('rows_pass', 1, 1), ('hop', 2, 1, 1, 2), ('cross', 0, 1, 4),
    ('hop', 2, 1, 0, 2), ('hop', 2, 0, 1, 3), ('hop', 2, 0, 0, 3), ('rows_pass', 2, 0), ('rows_pass', 2, 1),
    ('hop', 2, 1, 1, 3), ('hop', 2, 1, 0, 3), ('hop', 2, 0, 0, 4), ('rows_end',), ('siblings', 0), ('inner', 0, 0),
    ('hop', 2, 1, 1, 4), ('inner', 0, 1), ('siblings', 1), ('inner', 1, 0), ('inner', 1, 1), ('siblings', 2),
    ('inner', 2, 0), ('inner', 2, 1),
)
MESH = pl.DeviceIdType.MESH
F32 = jnp.float32
BF16 = jnp.bfloat16


def split_pair(values):
    upper = values.astype(BF16)
    return upper, (values - upper.astype(F32)).astype(BF16)


def kernel_body(
    x_ref, map_hbm, sign_hbm, blocks_hbm, sketch_ref, out_ref, map_ref, sign_ref, blocks_ref,
    mine, partner, summed_x, rx, raw, gath, rows, grad, wide, low, low_out, low_in, onehot, signs, stacked,
    local_sem, send_sem, ey_r, ex_r, el_r, sib_r, y2_r, yp_r, x_r, pass_r, z_r,
):
    group = lax.axis_index("group")
    x = lax.axis_index("shard")
    t = lax.axis_index("tensor")
    yh = group // (NZ * NC)
    z = lax.rem(group, NZ * NC) // NC
    c = lax.rem(group, NC)

    def at_group(yy, zz, cc):
        return {"group": (yy * NZ + zz) * NC + cc}

    sibling = at_group(yh, z, 1 - c)
    across = at_group(1 - yh, z, c)
    z_way = (at_group(yh, lax.rem(z + 1, NZ), c), at_group(yh, lax.rem(z + NZ - 1, NZ), c))
    other_term = {"tensor": 1 - t}

    def at_x(j):
        xx = lax.rem(x + j, NX)
        return xx, {"shard": xx}

    sent = [0, 0]

    def remote(src, dst, r, target, kind=0):
        copy = pltpu.make_async_remote_copy(
            src_ref=src, dst_ref=dst, send_sem=send_sem.at[kind], recv_sem=r, device_id=target, device_id_type=MESH
        )
        copy.start()
        sent[kind] += math.prod(src.shape) * (2 if src.dtype == F32 else 1)
        return copy

    def pieces(count):
        flat = gath.reshape(NZ * NC * NY * PART, ROWS, SKETCH)
        return flat.at[pl.ds(0, count)]

    def wait_pieces(sem, count):
        pltpu.make_async_copy(pieces(count), pieces(count), sem).wait()

    barrier = pltpu.get_barrier_semaphore()
    targets = [other_term, sibling, across, *z_way] + [at_x(j)[1] for j in (1, 2, 3)]
    for target in targets:
        pl.semaphore_signal(barrier, inc=1, device_id=target, device_id_type=MESH)
    pl.semaphore_wait(barrier, len(targets))

    def cut(p):
        return pl.ds(p * (SKETCH // CUTS), SKETCH // CUTS)

    def exchange(i, p):
        return remote(
            x_ref.at[:, 1 - t, i, :, cut(p)], partner.at[i, :, :, cut(p)], ey_r.at[i, p], other_term
        )

    def own_terms(i):
        copy = pltpu.make_async_copy(x_ref.at[:, t, i], mine.at[i], local_sem.at[i])
        copy.start()
        return copy

    def sum_terms(i, p, xx):
        return (mine[i, xx, :, cut(p)].astype(F32) + partner[i, xx, :, cut(p)].astype(F32)).astype(BF16)

    def along_shards(i, p):
        copies = []
        for j in (2, 1, 3):
            xx, target = at_x(j)
            summed_x[i, xx, :, cut(p)] = sum_terms(i, p, xx)
            copies.append(
                remote(
                    summed_x.at[i, xx, :, cut(p)], rx.at[i, x, :, cut(p)],
                    ex_r.at[i, p, j - 1], target,
                )
            )
        rx[i, x, :, cut(p)] = sum_terms(i, p, x)
        return copies

    def raw_along_shards(i, p):
        copies = []
        for j in (2, 1, 3):
            xx, target = at_x(j)
            copies.append(
                remote(
                    x_ref.at[xx, :, i, :, cut(p)], raw.at[i, x, :, :, cut(p)],
                    ex_r.at[i, p, j - 1], target,
                )
            )
        return copies

    def lay_out(source, p):
        each = SB // CUTS

        @pl.loop(0, NX)
        def _(xx):
            for b in range(p * each, (p + 1) * each):
                values = source(xx)[:, b * BLOCK:(b + 1) * BLOCK]
                grad[pl.ds(xx * SB + b, ROWS, stride=NX * SB), :] = values.astype(F32)

    def project(result):
        @pl.loop(0, ROWS // 2)
        def _(pair):
            parts = []
            for e in range(2):
                signed = grad[pl.ds(pl.multiple_of((pair * 2 + e) * BLOCK, BLOCK), BLOCK), :] * signs[...]
                parts.append(signed.astype(BF16))
            summed = jnp.dot(onehot[...], jnp.concatenate(parts, axis=1), preferred_element_type=F32)
            upper, lower = split_pair(summed)
            for e in range(2):
                place = pl.ds(pl.multiple_of((pair * 2 + e) * SB, SB), SB)
                cols = slice(e * BLOCK, (e + 1) * BLOCK)
                for f in range(FAN):
                    fr = slice(f * SB, (f + 1) * SB)
                    wide[place, f * BLOCK:(f + 1) * BLOCK] = upper[fr, cols]
                    wide[place, (FAN + f) * BLOCK:(FAN + f + 1) * BLOCK] = lower[fr, cols]

        result[...] = jnp.dot(wide[...], stacked[...], preferred_element_type=F32)

    def own_low(i):
        return low.at[pl.ds(i * ROWS * SB, ROWS * SB), :]

    def finish(i):
        for s in range(SB):
            piece = low[pl.ds(i * ROWS * SB + s, ROWS, stride=SB), :].astype(BF16)
            lanes = slice(s * BLOCK, (s + 1) * BLOCK)
            gath[z, c, yh, i, :, lanes] = piece
            rows[x, t, i, :, lanes] = piece
            sketch_ref[i * ROWS:(i + 1) * ROWS, lanes] = piece

    arrived_sibling = [0] * PART

    def to_sibling(i, block):
        arrived_sibling[i] += 1
        remote(block, block, sib_r.at[i], sibling, 1)

    from_z = {}
    from_across = {}
    from_rows = {}
    partner_rows = {}
    from_partner = {}
    from_x = {}
    low_from = {}
    own_copies = {}

    def to_across(i, w, h, block):
        from_across[i, w, h] = remote(block, block, y2_r.at[i, 0 if h == 0 else w * 3 + h], across)

    def round_z(i, k, w, h, block):
        from_z[i, k, w, h] = remote(block, block, z_r.at[i, k, w, h - 1], z_way[w])

    def place(w, h):
        return lax.rem(z + (NZ - h if w == 0 else h), NZ)

    def spread(i):
        own = gath.at[z, c, yh, i]
        for w in range(2):
            round_z(i, 0, w, 1, own)
        to_across(i, 0, 0, own)
        to_sibling(i, own)

    def relay(i):
        from_across[i, 0, 0].wait_recv()
        block = gath.at[z, c, 1 - yh, i]
        if not HALF[i]:
            for w in range(2):
                round_z(i, 1, w, 1, block)
        to_sibling(i, block)

    def hop(i, k, w, h):
        from_z[i, k, w, h].wait_recv()
        block = gath.at[place(w, h), c, yh if k == 0 else 1 - yh, i]
        if h < 3:
            round_z(i, k, w, h + 1, block)
        elif h == 3 and HALF[i]:
            round_z(i, k, w, 4, block.at[:, pl.ds(w * (SKETCH // 2), SKETCH // 2)])
        elif h == 3 and k == w:
            round_z(i, k, w, 4, block)
        if HALF[i] and h == 4 and w == 0:
            return
        if HALF[i]:
            to_across(i, w, h, block)
        to_sibling(i, block)

    def cross(i, w, h):
        from_across[i, w, h].wait_recv()
        to_sibling(i, gath.at[place(w, h), c, 1 - yh, i])

    def rows_begin(i):
        block = rows.at[x, t, i]
        partner_rows[i] = remote(block, block, yp_r.at[i], other_term)

    def rows_send(i):
        partner_rows[i].wait_recv()
        block = rows.at[x, :, i]
        for w, j in enumerate((1, 3)):
            from_rows[i, w] = remote(block, block, x_r.at[i, w], at_x(j)[1])

    def rows_pass(i, w):
        from_rows[i, w].wait_recv()
        j = (1, 3)[w]
        block = rows.at[at_x(4 - j)[0], t if w == 0 else 1 - t, i]
        remote(block, block, pass_r.at[0], at_x(j)[1])

    def rows_end():
        wait_pieces(pass_r.at[0], 2 * PART)

    def siblings(i):
        wait_pieces(sib_r.at[i], NZ * NY)

    def inner(i, q):
        left = gath[q * 4:(q + 1) * 4, :, :, i].reshape(4 * NC * NY * ROWS, SKETCH)
        right = rows[...].reshape(NX * NT * PART * ROWS, SKETCH)
        tile = lax.dot_general(left, right, (((1,), (1,)), ((), ())), preferred_element_type=F32) * (1.0 / SKETCH)
        tile = tile.reshape(4, NC, NY, ROWS, NX * NT * PART * ROWS)
        for a in range(4):
            for cc in range(NC):
                for yy in range(NY):
                    out_ref[yy, q * 4 + a, cc, i * ROWS:(i + 1) * ROWS, :] = tile[a, cc, yy]

    def begin(i):
        for p in range(CUTS):
            if RAW[i]:
                from_x[i, p] = raw_along_shards(i, p)
            else:
                from_partner[i, p] = exchange(i, p)
        if RAW[i]:
            own_copies[i] = pltpu.make_async_copy(x_ref.at[x, :, i], raw.at[i, x], local_sem.at[i])
        else:
            own_copies[i] = pltpu.make_async_copy(x_ref.at[:, t, i], mine.at[i], local_sem.at[i])
        own_copies[i].start()

    for i in range(FIRST):
        begin(i)
    small = []
    for k, (src, dst) in enumerate(((map_hbm, map_ref), (sign_hbm, sign_ref), (blocks_hbm, blocks_ref))):
        small.append(pltpu.make_async_copy(src, dst, local_sem.at[PART + k]))
        small[-1].start()
    for copy in small:
        copy.wait()

    goal = lax.broadcasted_iota(jnp.int32, (SB, BLOCK), 0)
    for f in range(FAN):
        onehot[f * SB:(f + 1) * SB, :] = jnp.where(map_ref[f:f + 1, :] == goal, 1.0, 0.0).astype(BF16)
        stacked[f * BLOCK:(f + 1) * BLOCK, :] = blocks_ref[f]
        stacked[(FAN + f) * BLOCK:(FAN + f + 1) * BLOCK, :] = blocks_ref[f]
    signs[...] = (2 * sign_ref[...] - 1).astype(F32)

    def terms(i, p):
        if p == 0:
            own_copies[i].wait()
        from_partner[i, p].wait_recv()
        from_x[i, p] = along_shards(i, p)

    def sketch(i):
        for p in range(CUTS):
            for copy in from_x[i, p]:
                copy.wait_recv()
            lay_out(lambda xx: rx.at[i, xx], p)
        project(own_low(i))
        finish(i)
        spread(i)

    def raw_sketch(i):
        own_copies[i].wait()
        for p in range(CUTS):
            for copy in from_x[i, p]:
                copy.wait_recv()
            lay_out(lambda xx: raw.at[i, xx, 1 - t], p)
        project(low_out.at[i])
        low_from[i] = remote(low_out.at[i], low_in.at[i], el_r.at[i], other_term)
        for p in range(CUTS):
            lay_out(lambda xx: raw.at[i, xx, t], p)
        project(own_low(i))

    def raw_finish(i):
        low_from[i].wait_recv()
        own_low(i)[...] = own_low(i)[...] + low_in[i]
        finish(i)
        spread(i)

    steps = {
        "begin": begin, "terms": terms, "sketch": sketch, "raw_sketch": raw_sketch, "raw_finish": raw_finish,
        "relay": relay, "hop": hop, "cross": cross, "rows_begin": rows_begin, "rows_send": rows_send,
        "rows_pass": rows_pass, "rows_end": rows_end, "siblings": siblings, "inner": inner,
    }
    for step in ORDER:
        steps[step[0]](*step[1:])

    for kind in range(2):
        wait_pieces(send_sem.at[kind], sent[kind] // (ROWS * SKETCH))


def on_device(partials, index_map, sign_bits, blocks):
    count = NX * NT * PART * ROWS
    piece = (ROWS, SKETCH)
    dma = pltpu.SemaphoreType.DMA
    vmem = pl.BlockSpec(memory_space=pltpu.VMEM)
    sketch, kernel = pl.pallas_call(
        kernel_body,
        out_shape=(
            pltpu.VMEM((PART * ROWS, SKETCH), BF16),
            pltpu.VMEM((NY, NZ, NC, PART * ROWS, count), F32),
        ),
        in_specs=[pl.BlockSpec(memory_space=pltpu.HBM)] * 4,
        out_specs=(vmem, vmem),
        scratch_shapes=[
            pltpu.VMEM(index_map.shape[::-1], jnp.int32),
            pltpu.VMEM((BLOCK, BLOCK), jnp.int32),
            pltpu.VMEM(blocks.shape, BF16),
            pltpu.VMEM((PART, NX) + piece, BF16),
            pltpu.VMEM((PART, NX) + piece, BF16),
            pltpu.VMEM((PART, NX) + piece, BF16),
            pltpu.VMEM((PART, NX) + piece, BF16),
            pltpu.VMEM((PART, NX, NT) + piece, BF16),
            pltpu.VMEM((NZ, NC, NY, PART) + piece, BF16),
            pltpu.VMEM((NX, NT, PART) + piece, BF16),
            pltpu.VMEM((ROWS * BLOCK, BLOCK), F32),
            pltpu.VMEM((ROWS * SB, 2 * FAN * BLOCK), BF16),
            pltpu.VMEM((PART * ROWS * SB, BLOCK), F32),
            pltpu.VMEM((PART, ROWS * SB, BLOCK), F32),
            pltpu.VMEM((PART, ROWS * SB, BLOCK), F32),
            pltpu.VMEM((FAN * SB, BLOCK), BF16),
            pltpu.VMEM((BLOCK, BLOCK), F32),
            pltpu.VMEM((2 * FAN * BLOCK, BLOCK), BF16),
            dma((PART + 3,)), dma((2,)),
            dma((PART, CUTS)), dma((PART, CUTS, 3)), dma((PART,)), dma((PART,)),
            dma((PART, 8)), dma((PART,)), dma((PART, 2)), dma((1,)), dma((PART, 2, 2, 4)),
        ],
        compiler_params=pltpu.CompilerParams(
            collective_id=0, has_side_effects=True, vmem_limit_bytes=56 * 2**20
        ),
        cost_estimate=pl.CostEstimate(flops=6 * 10**9, bytes_accessed=6 * 10**6, transcendentals=0),
        name="sketch_kernel",
    )(
        partials.reshape(NX, NT, PART, ROWS, -1),
        index_map.T,
        sign_bits.reshape(BLOCK, BLOCK),
        blocks,
    )
    return sketch, kernel.reshape(NY * NZ * NC, PART * ROWS, count)


def solution(mesh):
    placed = (P("group", "tensor", "shard"), P(), P(), P())
    return jax.shard_map(
        on_device,
        mesh=mesh,
        in_specs=placed,
        out_specs=(P(("group", "shard", "tensor"), None), P(None, ("shard", "tensor"), "group")),
        check_vma=False,
    )
```

```python
import math

import jax
import jax.numpy as jnp
from jax import lax
from jax.experimental import pallas as pl
from jax.experimental.pallas import tpu as pltpu
from jax.sharding import PartitionSpec as P

SKETCH = 4096
BLOCK = 128
FAN = 4
SB = SKETCH // BLOCK
NX, NT, NZ, NY, NC = 4, 2, 8, 2, 2
PART = 3
ROWS = 16
CUTS = 4
HALF = (True, False, False)
RAW = (False, True, False)
FIRST = 2
ORDER = (
    ('terms', 0, 0), ('terms', 0, 1), ('terms', 0, 2), ('terms', 0, 3), ('begin', 2), ('raw_sketch', 1),
    ('sketch', 0), ('terms', 2, 0), ('terms', 2, 1), ('terms', 2, 2), ('terms', 2, 3), ('rows_begin', 0),
    ('hop', 0, 0, 0, 1), ('hop', 0, 0, 1, 1), ('sketch', 2), ('raw_finish', 1), ('rows_begin', 1),
    ('rows_begin', 2), ('hop', 0, 0, 0, 2), ('hop', 0, 0, 1, 2), ('relay', 0), ('rows_send', 0),
    ('hop', 2, 0, 0, 1), ('hop', 2, 0, 1, 1), ('cross', 0, 0, 1), ('hop', 1, 0, 1, 1), ('hop', 1, 0, 0, 1),
    ('cross', 0, 1, 1), ('rows_pass', 0, 0), ('rows_pass', 0, 1), ('hop', 0, 0, 0, 3), ('hop', 0, 0, 1, 3),
    ('relay', 2), ('hop', 2, 0, 0, 2), ('hop', 2, 0, 1, 2), ('relay', 1), ('hop', 1, 0, 1, 2), ('hop', 1, 0, 0, 2),
    ('hop', 0, 0, 0, 4), ('hop', 0, 0, 1, 4), ('rows_send', 1), ('hop', 2, 1, 1, 1), ('hop', 2, 1, 0, 1),
    ('rows_send', 2), ('hop', 2, 0, 0, 3), ('hop', 2, 0, 1, 3), ('cross', 0, 0, 2), ('rows_pass', 1, 1),
    ('rows_pass', 1, 0), ('hop', 1, 1, 1, 1), ('hop', 1, 1, 0, 1), ('cross', 0, 1, 2), ('hop', 1, 0, 1, 3),
    ('hop', 1, 0, 0, 3), ('cross', 0, 0, 3), ('rows_pass', 2, 1), ('rows_pass', 2, 0), ('hop', 2, 1, 1, 2),
    ('hop', 2, 1, 0, 2), ('cross', 0, 1, 3), ('hop', 1, 1, 1, 2), ('hop', 2, 0, 0, 4), ('cross', 0, 1, 4),
    ('rows_end',), ('inner', 0, 0), ('hop', 1, 1, 0, 2), ('hop', 2, 1, 1, 3), ('inner', 0, 1), ('inner', 1, 0),
    ('hop', 1, 1, 1, 3), ('hop', 1, 0, 0, 4), ('inner', 2, 0), ('hop', 2, 1, 0, 3), ('hop', 2, 1, 1, 4),
    ('inner', 2, 1), ('hop', 1, 1, 0, 3), ('hop', 1, 1, 1, 4), ('inner', 1, 1),
)
MESH = pl.DeviceIdType.MESH
F32 = jnp.float32
BF16 = jnp.bfloat16


def split_pair(values):
    upper = values.astype(BF16)
    return upper, (values - upper.astype(F32)).astype(BF16)


def kernel_body(
    x_ref, map_hbm, sign_hbm, blocks_hbm, sketch_ref, out_ref, map_ref, sign_ref, blocks_ref,
    mine, partner, summed_x, rx, raw, gath, rows, grad, wide, low, low_out, low_in, onehot, signs, stacked,
    local_sem, send_sem, ey_r, ex_r, el_r, sib_r, y2_r, yp_r, x_r, pass_r, z_r,
):
    group = lax.axis_index("group")
    x = lax.axis_index("shard")
    t = lax.axis_index("tensor")
    yh = group // (NZ * NC)
    z = lax.rem(group, NZ * NC) // NC
    c = lax.rem(group, NC)

    def at_group(yy, zz, cc):
        return {"group": (yy * NZ + zz) * NC + cc}

    sibling = at_group(yh, z, 1 - c)
    across = at_group(1 - yh, z, c)
    z_way = (at_group(yh, lax.rem(z + 1, NZ), c), at_group(yh, lax.rem(z + NZ - 1, NZ), c))
    other_term = {"tensor": 1 - t}

    def at_x(j):
        xx = lax.rem(x + j, NX)
        return xx, {"shard": xx}

    sent = [0, 0]

    def remote(src, dst, r, target, kind=0):
        copy = pltpu.make_async_remote_copy(
            src_ref=src, dst_ref=dst, send_sem=send_sem.at[kind], recv_sem=r, device_id=target, device_id_type=MESH
        )
        copy.start()
        sent[kind] += math.prod(src.shape) * (2 if src.dtype == F32 else 1)
        return copy

    def pieces(count):
        flat = gath.reshape(NZ * NC * NY * PART, ROWS, SKETCH)
        return flat.at[pl.ds(0, count)]

    def wait_pieces(sem, count):
        pltpu.make_async_copy(pieces(count), pieces(count), sem).wait()

    barrier = pltpu.get_barrier_semaphore()
    targets = [other_term, sibling, across, *z_way] + [at_x(j)[1] for j in (1, 2, 3)]
    for target in targets:
        pl.semaphore_signal(barrier, inc=1, device_id=target, device_id_type=MESH)
    pl.semaphore_wait(barrier, len(targets))

    def cut(p):
        return pl.ds(p * (SKETCH // CUTS), SKETCH // CUTS)

    def exchange(i, p):
        return remote(
            x_ref.at[:, 1 - t, i, :, cut(p)], partner.at[i, :, :, cut(p)], ey_r.at[i, p], other_term
        )

    def own_terms(i):
        copy = pltpu.make_async_copy(x_ref.at[:, t, i], mine.at[i], local_sem.at[i])
        copy.start()
        return copy

    def sum_terms(i, p, xx):
        return (mine[i, xx, :, cut(p)].astype(F32) + partner[i, xx, :, cut(p)].astype(F32)).astype(BF16)

    def along_shards(i, p):
        copies = []
        for j in (2, 1, 3):
            xx, target = at_x(j)
            summed_x[i, xx, :, cut(p)] = sum_terms(i, p, xx)
            copies.append(
                remote(
                    summed_x.at[i, xx, :, cut(p)], rx.at[i, x, :, cut(p)],
                    ex_r.at[i, p, j - 1], target,
                )
            )
        rx[i, x, :, cut(p)] = sum_terms(i, p, x)
        return copies

    def raw_along_shards(i, p):
        copies = []
        for j in (2, 1, 3):
            xx, target = at_x(j)
            copies.append(
                remote(
                    x_ref.at[xx, :, i, :, cut(p)], raw.at[i, x, :, :, cut(p)],
                    ex_r.at[i, p, j - 1], target,
                )
            )
        return copies

    def lay_out(source, p):
        each = SB // CUTS

        @pl.loop(0, NX)
        def _(xx):
            for b in range(p * each, (p + 1) * each):
                values = source(xx)[:, b * BLOCK:(b + 1) * BLOCK]
                grad[pl.ds(xx * SB + b, ROWS, stride=NX * SB), :] = values.astype(F32)

    def project(result):
        @pl.loop(0, ROWS // 2)
        def _(pair):
            parts = []
            for e in range(2):
                signed = grad[pl.ds(pl.multiple_of((pair * 2 + e) * BLOCK, BLOCK), BLOCK), :] * signs[...]
                parts.append(signed.astype(BF16))
            summed = jnp.dot(onehot[...], jnp.concatenate(parts, axis=1), preferred_element_type=F32)
            upper, lower = split_pair(summed)
            for e in range(2):
                place = pl.ds(pl.multiple_of((pair * 2 + e) * SB, SB), SB)
                cols = slice(e * BLOCK, (e + 1) * BLOCK)
                for f in range(FAN):
                    fr = slice(f * SB, (f + 1) * SB)
                    wide[place, f * BLOCK:(f + 1) * BLOCK] = upper[fr, cols]
                    wide[place, (FAN + f) * BLOCK:(FAN + f + 1) * BLOCK] = lower[fr, cols]

        result[...] = jnp.dot(wide[...], stacked[...], preferred_element_type=F32)

    def own_low(i):
        return low.at[pl.ds(i * ROWS * SB, ROWS * SB), :]

    def finish(i):
        for s in range(SB):
            piece = low[pl.ds(i * ROWS * SB + s, ROWS, stride=SB), :].astype(BF16)
            lanes = slice(s * BLOCK, (s + 1) * BLOCK)
            gath[z, c, yh, i, :, lanes] = piece
            rows[x, t, i, :, lanes] = piece
            sketch_ref[i * ROWS:(i + 1) * ROWS, lanes] = piece

    def to_sibling(i, block, h):
        remote(block, block, sib_r.at[i, 0 if h < 3 else 1], sibling, 1)

    from_z = {}
    from_across = {}
    from_rows = {}
    partner_rows = {}
    from_partner = {}
    from_x = {}
    low_from = {}
    own_copies = {}

    def to_across(i, w, h, block):
        from_across[i, w, h] = remote(block, block, y2_r.at[i, 0 if h == 0 else w * 3 + h], across)

    def round_z(i, k, w, h, block):
        from_z[i, k, w, h] = remote(block, block, z_r.at[i, k, w, h - 1], z_way[w])

    def place(w, h):
        return lax.rem(z + (NZ - h if w == 0 else h), NZ)

    def spread(i):
        own = gath.at[z, c, yh, i]
        for w in range(2):
            round_z(i, 0, w, 1, own)
        to_across(i, 0, 0, own)
        to_sibling(i, own, 0)

    def relay(i):
        from_across[i, 0, 0].wait_recv()
        block = gath.at[z, c, 1 - yh, i]
        if not HALF[i]:
            for w in range(2):
                round_z(i, 1, w, 1, block)
        to_sibling(i, block, 0)

    def hop(i, k, w, h):
        from_z[i, k, w, h].wait_recv()
        block = gath.at[place(w, h), c, yh if k == 0 else 1 - yh, i]
        if h < 3:
            round_z(i, k, w, h + 1, block)
        elif h == 3 and HALF[i]:
            round_z(i, k, w, 4, block.at[:, pl.ds(w * (SKETCH // 2), SKETCH // 2)])
        elif h == 3 and k == w:
            round_z(i, k, w, 4, block)
        if HALF[i] and h == 4 and w == 0:
            return
        if HALF[i]:
            to_across(i, w, h, block)
        to_sibling(i, block, h)

    def cross(i, w, h):
        from_across[i, w, h].wait_recv()
        to_sibling(i, gath.at[place(w, h), c, 1 - yh, i], h)

    def rows_begin(i):
        block = rows.at[x, t, i]
        partner_rows[i] = remote(block, block, yp_r.at[i], other_term)

    def rows_send(i):
        partner_rows[i].wait_recv()
        block = rows.at[x, :, i]
        for w, j in enumerate((1, 3)):
            from_rows[i, w] = remote(block, block, x_r.at[i, w], at_x(j)[1])

    def rows_pass(i, w):
        from_rows[i, w].wait_recv()
        j = (1, 3)[w]
        block = rows.at[at_x(4 - j)[0], t if w == 0 else 1 - t, i]
        remote(block, block, pass_r.at[0], at_x(j)[1])

    def rows_end():
        wait_pieces(pass_r.at[0], 2 * PART)

    def inner(i, late):
        wait_pieces(sib_r.at[i, late], (10, 6)[late])
        turns = ((0, 1, 7, 2, 6), (3, 5, 4))[late]
        spots = [lax.rem(z + turn, NZ) for turn in turns]
        left = jnp.concatenate([gath[zz, :, :, i].reshape(NC * NY * ROWS, SKETCH) for zz in spots], axis=0)
        right = rows[...].reshape(NX * NT * PART * ROWS, SKETCH)
        tile = lax.dot_general(left, right, (((1,), (1,)), ((), ())), preferred_element_type=F32) * (1.0 / SKETCH)
        tile = tile.reshape(len(turns), NC, NY, ROWS, NX * NT * PART * ROWS)
        for a, zz in enumerate(spots):
            for cc in range(NC):
                for yy in range(NY):
                    out_ref[yy, zz, cc, i * ROWS:(i + 1) * ROWS, :] = tile[a, cc, yy]

    def begin(i):
        for p in range(CUTS):
            if RAW[i]:
                from_x[i, p] = raw_along_shards(i, p)
            else:
                from_partner[i, p] = exchange(i, p)
        if RAW[i]:
            own_copies[i] = pltpu.make_async_copy(x_ref.at[x, :, i], raw.at[i, x], local_sem.at[i])
        else:
            own_copies[i] = pltpu.make_async_copy(x_ref.at[:, t, i], mine.at[i], local_sem.at[i])
        own_copies[i].start()

    for i in range(FIRST):
        begin(i)
    small = []
    for k, (src, dst) in enumerate(((map_hbm, map_ref), (sign_hbm, sign_ref), (blocks_hbm, blocks_ref))):
        small.append(pltpu.make_async_copy(src, dst, local_sem.at[PART + k]))
        small[-1].start()
    for copy in small:
        copy.wait()

    goal = lax.broadcasted_iota(jnp.int32, (SB, BLOCK), 0)
    for f in range(FAN):
        onehot[f * SB:(f + 1) * SB, :] = jnp.where(map_ref[f:f + 1, :] == goal, 1.0, 0.0).astype(BF16)
        stacked[f * BLOCK:(f + 1) * BLOCK, :] = blocks_ref[f]
        stacked[(FAN + f) * BLOCK:(FAN + f + 1) * BLOCK, :] = blocks_ref[f]
    signs[...] = (2 * sign_ref[...] - 1).astype(F32)

    def terms(i, p):
        if p == 0:
            own_copies[i].wait()
        from_partner[i, p].wait_recv()
        from_x[i, p] = along_shards(i, p)

    def sketch(i):
        for p in range(CUTS):
            for copy in from_x[i, p]:
                copy.wait_recv()
            lay_out(lambda xx: rx.at[i, xx], p)
        project(own_low(i))
        finish(i)
        spread(i)

    def raw_sketch(i):
        own_copies[i].wait()
        for p in range(CUTS):
            for copy in from_x[i, p]:
                copy.wait_recv()
            lay_out(lambda xx: raw.at[i, xx, 1 - t], p)
        project(low_out.at[i])
        low_from[i] = remote(low_out.at[i], low_in.at[i], el_r.at[i], other_term)
        for p in range(CUTS):
            lay_out(lambda xx: raw.at[i, xx, t], p)
        project(own_low(i))

    def raw_finish(i):
        low_from[i].wait_recv()
        own_low(i)[...] = own_low(i)[...] + low_in[i]
        finish(i)
        spread(i)

    steps = {
        "begin": begin, "terms": terms, "sketch": sketch, "raw_sketch": raw_sketch, "raw_finish": raw_finish,
        "relay": relay, "hop": hop, "cross": cross, "rows_begin": rows_begin, "rows_send": rows_send,
        "rows_pass": rows_pass, "rows_end": rows_end, "inner": inner,
    }
    for step in ORDER:
        steps[step[0]](*step[1:])

    for kind in range(2):
        wait_pieces(send_sem.at[kind], sent[kind] // (ROWS * SKETCH))


def on_device(partials, index_map, sign_bits, blocks):
    count = NX * NT * PART * ROWS
    piece = (ROWS, SKETCH)
    dma = pltpu.SemaphoreType.DMA
    vmem = pl.BlockSpec(memory_space=pltpu.VMEM)
    sketch, kernel = pl.pallas_call(
        kernel_body,
        out_shape=(
            pltpu.VMEM((PART * ROWS, SKETCH), BF16),
            pltpu.VMEM((NY, NZ, NC, PART * ROWS, count), F32),
        ),
        in_specs=[pl.BlockSpec(memory_space=pltpu.HBM)] * 4,
        out_specs=(vmem, vmem),
        scratch_shapes=[
            pltpu.VMEM(index_map.shape[::-1], jnp.int32),
            pltpu.VMEM((BLOCK, BLOCK), jnp.int32),
            pltpu.VMEM(blocks.shape, BF16),
            pltpu.VMEM((PART, NX) + piece, BF16),
            pltpu.VMEM((PART, NX) + piece, BF16),
            pltpu.VMEM((PART, NX) + piece, BF16),
            pltpu.VMEM((PART, NX) + piece, BF16),
            pltpu.VMEM((PART, NX, NT) + piece, BF16),
            pltpu.VMEM((NZ, NC, NY, PART) + piece, BF16),
            pltpu.VMEM((NX, NT, PART) + piece, BF16),
            pltpu.VMEM((ROWS * BLOCK, BLOCK), F32),
            pltpu.VMEM((ROWS * SB, 2 * FAN * BLOCK), BF16),
            pltpu.VMEM((PART * ROWS * SB, BLOCK), F32),
            pltpu.VMEM((PART, ROWS * SB, BLOCK), F32),
            pltpu.VMEM((PART, ROWS * SB, BLOCK), F32),
            pltpu.VMEM((FAN * SB, BLOCK), BF16),
            pltpu.VMEM((BLOCK, BLOCK), F32),
            pltpu.VMEM((2 * FAN * BLOCK, BLOCK), BF16),
            dma((PART + 3,)), dma((2,)),
            dma((PART, CUTS)), dma((PART, CUTS, 3)), dma((PART,)),
            dma((PART, 2)), dma((PART, 8)), dma((PART,)), dma((PART, 2)), dma((1,)), dma((PART, 2, 2, 4)),
        ],
        compiler_params=pltpu.CompilerParams(
            collective_id=0, has_side_effects=True, vmem_limit_bytes=56 * 2**20
        ),
        cost_estimate=pl.CostEstimate(flops=6 * 10**9, bytes_accessed=6 * 10**6, transcendentals=0),
        name="sketch_kernel",
    )(
        partials.reshape(NX, NT, PART, ROWS, -1),
        index_map.T,
        sign_bits.reshape(BLOCK, BLOCK),
        blocks,
    )
    return sketch, kernel.reshape(NY * NZ * NC, PART * ROWS, count)


def solution(mesh):
    placed = (P("group", "tensor", "shard"), P(), P(), P())
    return jax.shard_map(
        on_device,
        mesh=mesh,
        in_specs=placed,
        out_specs=(P(("group", "shard", "tensor"), None), P(None, ("shard", "tensor"), "group")),
        check_vma=False,
    )
```

```python
import math

import jax
import jax.numpy as jnp
from jax import lax
from jax.experimental import pallas as pl
from jax.experimental.pallas import tpu as pltpu
from jax.sharding import PartitionSpec as P

SKETCH = 4096
BLOCK = 128
FAN = 4
SB = SKETCH // BLOCK
NX, NT, NZ, NY, NC = 4, 2, 8, 2, 2
PART = 3
ROWS = 16
CUTS = 4
HALF = (True, False, False)
RAW = (False, False, True)
FIRST = 1
ORDER = (
    ('begin', 2), ('terms', 0, 0), ('terms', 0, 1), ('terms', 0, 2), ('terms', 0, 3), ('begin', 1),
    ('raw_sketch', 2), ('raw_own', 2), ('terms', 1, 0), ('terms', 1, 1), ('sketch', 0), ('terms', 1, 2),
    ('terms', 1, 3), ('rows_begin', 0), ('hop', 0, 0, 0, 1), ('hop', 0, 0, 1, 1), ('sketch', 1), ('raw_finish', 2),
    ('rows_begin', 1), ('rows_begin', 2), ('hop', 0, 0, 1, 2), ('hop', 0, 0, 0, 2), ('relay', 0), ('rows_send', 0),
    ('hop', 1, 0, 1, 1), ('hop', 1, 0, 0, 1), ('cross', 0, 0, 1), ('hop', 2, 0, 0, 1), ('hop', 2, 0, 1, 1),
    ('cross', 0, 1, 1), ('rows_pass', 0, 0), ('rows_pass', 0, 1), ('hop', 0, 0, 1, 3), ('hop', 0, 0, 0, 3),
    ('relay', 1), ('hop', 1, 0, 1, 2), ('hop', 1, 0, 0, 2), ('relay', 2), ('hop', 2, 0, 1, 2), ('hop', 2, 0, 0, 2),
    ('hop', 0, 0, 0, 4), ('hop', 0, 0, 1, 4), ('rows_send', 1), ('hop', 1, 1, 0, 1), ('hop', 1, 1, 1, 1),
    ('rows_send', 2), ('hop', 1, 0, 1, 3), ('hop', 1, 0, 0, 3), ('cross', 0, 1, 2), ('rows_pass', 1, 1),
    ('rows_pass', 1, 0), ('hop', 2, 1, 0, 1), ('hop', 2, 1, 1, 1), ('cross', 0, 0, 2), ('hop', 2, 0, 0, 3),
    ('hop', 2, 0, 1, 3), ('cross', 0, 1, 3), ('rows_pass', 2, 0), ('rows_pass', 2, 1), ('hop', 1, 1, 0, 2),
    ('hop', 1, 1, 1, 2), ('cross', 0, 0, 3), ('hop', 1, 0, 0, 4), ('hop', 2, 1, 1, 2), ('cross', 0, 1, 4),
    ('rows_end',), ('inner', 0, 0), ('hop', 1, 1, 1, 3), ('hop', 2, 1, 0, 2), ('inner', 0, 1), ('inner', 1, 0),
    ('hop', 2, 1, 1, 3), ('hop', 2, 0, 0, 4), ('inner', 2, 0), ('hop', 1, 1, 0, 3), ('hop', 1, 1, 1, 4),
    ('inner', 1, 1), ('hop', 2, 1, 0, 3), ('hop', 2, 1, 1, 4), ('inner', 2, 1),
)
MESH = pl.DeviceIdType.MESH
F32 = jnp.float32
BF16 = jnp.bfloat16


def split_pair(values):
    upper = values.astype(BF16)
    return upper, (values - upper.astype(F32)).astype(BF16)


def kernel_body(
    x_ref, map_hbm, sign_hbm, blocks_hbm, sketch_ref, out_ref, map_ref, sign_ref, blocks_ref,
    mine, partner, summed_x, rx, raw, gath, rows, grad, wide, low, low_out, low_in, onehot, signs, stacked,
    local_sem, send_sem, ey_r, ex_r, el_r, sib_r, y2_r, yp_r, x_r, pass_r, z_r,
):
    group = lax.axis_index("group")
    x = lax.axis_index("shard")
    t = lax.axis_index("tensor")
    yh = group // (NZ * NC)
    z = lax.rem(group, NZ * NC) // NC
    c = lax.rem(group, NC)

    def at_group(yy, zz, cc):
        return {"group": (yy * NZ + zz) * NC + cc}

    sibling = at_group(yh, z, 1 - c)
    across = at_group(1 - yh, z, c)
    z_way = (at_group(yh, lax.rem(z + 1, NZ), c), at_group(yh, lax.rem(z + NZ - 1, NZ), c))
    other_term = {"tensor": 1 - t}

    def at_x(j):
        xx = lax.rem(x + j, NX)
        return xx, {"shard": xx}

    sent = [0, 0]

    def remote(src, dst, r, target, kind=0):
        copy = pltpu.make_async_remote_copy(
            src_ref=src, dst_ref=dst, send_sem=send_sem.at[kind], recv_sem=r, device_id=target, device_id_type=MESH
        )
        copy.start()
        sent[kind] += math.prod(src.shape) * (2 if src.dtype == F32 else 1)
        return copy

    def pieces(count):
        flat = gath.reshape(NZ * NC * NY * PART, ROWS, SKETCH)
        return flat.at[pl.ds(0, count)]

    def wait_pieces(sem, count):
        pltpu.make_async_copy(pieces(count), pieces(count), sem).wait()

    barrier = pltpu.get_barrier_semaphore()
    targets = [other_term, sibling, across, *z_way] + [at_x(j)[1] for j in (1, 2, 3)]
    for target in targets:
        pl.semaphore_signal(barrier, inc=1, device_id=target, device_id_type=MESH)
    pl.semaphore_wait(barrier, len(targets))

    def cut(p):
        return pl.ds(p * (SKETCH // CUTS), SKETCH // CUTS)

    def exchange(i, p):
        return remote(
            x_ref.at[:, 1 - t, i, :, cut(p)], partner.at[i, :, :, cut(p)], ey_r.at[i, p], other_term
        )

    def own_terms(i):
        copy = pltpu.make_async_copy(x_ref.at[:, t, i], mine.at[i], local_sem.at[i])
        copy.start()
        return copy

    def sum_terms(i, p, xx):
        return (mine[i, xx, :, cut(p)].astype(F32) + partner[i, xx, :, cut(p)].astype(F32)).astype(BF16)

    def along_shards(i, p):
        copies = []
        for j in (2, 1, 3):
            xx, target = at_x(j)
            summed_x[i, xx, :, cut(p)] = sum_terms(i, p, xx)
            copies.append(
                remote(
                    summed_x.at[i, xx, :, cut(p)], rx.at[i, x, :, cut(p)],
                    ex_r.at[i, p, j - 1], target,
                )
            )
        rx[i, x, :, cut(p)] = sum_terms(i, p, x)
        return copies

    def raw_along_shards(i, p):
        copies = []
        for j in (2, 1, 3):
            xx, target = at_x(j)
            copies.append(
                remote(
                    x_ref.at[xx, :, i, :, cut(p)], raw.at[i, x, :, :, cut(p)],
                    ex_r.at[i, p, j - 1], target,
                )
            )
        return copies

    def lay_out(source, p):
        each = SB // CUTS

        @pl.loop(0, NX)
        def _(xx):
            for b in range(p * each, (p + 1) * each):
                values = source(xx)[:, b * BLOCK:(b + 1) * BLOCK]
                grad[pl.ds(xx * SB + b, ROWS, stride=NX * SB), :] = values.astype(F32)

    def project(result):
        @pl.loop(0, ROWS // 2)
        def _(pair):
            parts = []
            for e in range(2):
                signed = grad[pl.ds(pl.multiple_of((pair * 2 + e) * BLOCK, BLOCK), BLOCK), :] * signs[...]
                parts.append(signed.astype(BF16))
            summed = jnp.dot(onehot[...], jnp.concatenate(parts, axis=1), preferred_element_type=F32)
            upper, lower = split_pair(summed)
            for e in range(2):
                place = pl.ds(pl.multiple_of((pair * 2 + e) * SB, SB), SB)
                cols = slice(e * BLOCK, (e + 1) * BLOCK)
                for f in range(FAN):
                    fr = slice(f * SB, (f + 1) * SB)
                    wide[place, f * BLOCK:(f + 1) * BLOCK] = upper[fr, cols]
                    wide[place, (FAN + f) * BLOCK:(FAN + f + 1) * BLOCK] = lower[fr, cols]

        result[...] = jnp.dot(wide[...], stacked[...], preferred_element_type=F32)

    def own_low(i):
        return low.at[pl.ds(i * ROWS * SB, ROWS * SB), :]

    def finish(i):
        for s in range(SB):
            piece = low[pl.ds(i * ROWS * SB + s, ROWS, stride=SB), :].astype(BF16)
            lanes = slice(s * BLOCK, (s + 1) * BLOCK)
            gath[z, c, yh, i, :, lanes] = piece
            rows[x, t, i, :, lanes] = piece
            sketch_ref[i * ROWS:(i + 1) * ROWS, lanes] = piece

    def to_sibling(i, block, h):
        remote(block, block, sib_r.at[i, 0 if h < 3 else 1], sibling, 1)

    from_z = {}
    from_across = {}
    from_rows = {}
    partner_rows = {}
    from_partner = {}
    from_x = {}
    low_from = {}
    own_copies = {}

    def to_across(i, w, h, block):
        from_across[i, w, h] = remote(block, block, y2_r.at[i, 0 if h == 0 else w * 3 + h], across)

    def round_z(i, k, w, h, block):
        from_z[i, k, w, h] = remote(block, block, z_r.at[i, k, w, h - 1], z_way[w])

    def place(w, h):
        return lax.rem(z + (NZ - h if w == 0 else h), NZ)

    def spread(i):
        own = gath.at[z, c, yh, i]
        for w in range(2):
            round_z(i, 0, w, 1, own)
        to_across(i, 0, 0, own)
        to_sibling(i, own, 0)

    def relay(i):
        from_across[i, 0, 0].wait_recv()
        block = gath.at[z, c, 1 - yh, i]
        if not HALF[i]:
            for w in range(2):
                round_z(i, 1, w, 1, block)
        to_sibling(i, block, 0)

    def hop(i, k, w, h):
        from_z[i, k, w, h].wait_recv()
        block = gath.at[place(w, h), c, yh if k == 0 else 1 - yh, i]
        if h < 3:
            round_z(i, k, w, h + 1, block)
        elif h == 3 and HALF[i]:
            round_z(i, k, w, 4, block.at[:, pl.ds(w * (SKETCH // 2), SKETCH // 2)])
        elif h == 3 and k == w:
            round_z(i, k, w, 4, block)
        if HALF[i] and h == 4 and w == 0:
            return
        if HALF[i]:
            to_across(i, w, h, block)
        to_sibling(i, block, h)

    def cross(i, w, h):
        from_across[i, w, h].wait_recv()
        to_sibling(i, gath.at[place(w, h), c, 1 - yh, i], h)

    def rows_begin(i):
        block = rows.at[x, t, i]
        partner_rows[i] = remote(block, block, yp_r.at[i], other_term)

    def rows_send(i):
        partner_rows[i].wait_recv()
        block = rows.at[x, :, i]
        for w, j in enumerate((1, 3)):
            from_rows[i, w] = remote(block, block, x_r.at[i, w], at_x(j)[1])

    def rows_pass(i, w):
        from_rows[i, w].wait_recv()
        j = (1, 3)[w]
        block = rows.at[at_x(4 - j)[0], t if w == 0 else 1 - t, i]
        remote(block, block, pass_r.at[0], at_x(j)[1])

    def rows_end():
        wait_pieces(pass_r.at[0], 2 * PART)

    def inner(i, late):
        wait_pieces(sib_r.at[i, late], (10, 6)[late])
        turns = ((0, 1, 7, 2, 6), (3, 5, 4))[late]
        spots = [lax.rem(z + turn, NZ) for turn in turns]
        left = jnp.concatenate([gath[zz, :, :, i].reshape(NC * NY * ROWS, SKETCH) for zz in spots], axis=0)
        right = rows[...].reshape(NX * NT * PART * ROWS, SKETCH)
        tile = lax.dot_general(left, right, (((1,), (1,)), ((), ())), preferred_element_type=F32) * (1.0 / SKETCH)
        tile = tile.reshape(len(turns), NC, NY, ROWS, NX * NT * PART * ROWS)
        for a, zz in enumerate(spots):
            for cc in range(NC):
                for yy in range(NY):
                    out_ref[yy, zz, cc, i * ROWS:(i + 1) * ROWS, :] = tile[a, cc, yy]

    def begin(i):
        for p in range(CUTS):
            if RAW[i]:
                from_x[i, p] = raw_along_shards(i, p)
            else:
                from_partner[i, p] = exchange(i, p)
        if RAW[i]:
            own_copies[i] = pltpu.make_async_copy(x_ref.at[x, :, i], raw.at[i, x], local_sem.at[i])
        else:
            own_copies[i] = pltpu.make_async_copy(x_ref.at[:, t, i], mine.at[i], local_sem.at[i])
        own_copies[i].start()

    for i in range(FIRST):
        begin(i)
    small = []
    for k, (src, dst) in enumerate(((map_hbm, map_ref), (sign_hbm, sign_ref), (blocks_hbm, blocks_ref))):
        small.append(pltpu.make_async_copy(src, dst, local_sem.at[PART + k]))
        small[-1].start()
    for copy in small:
        copy.wait()

    goal = lax.broadcasted_iota(jnp.int32, (SB, BLOCK), 0)
    for f in range(FAN):
        onehot[f * SB:(f + 1) * SB, :] = jnp.where(map_ref[f:f + 1, :] == goal, 1.0, 0.0).astype(BF16)
        stacked[f * BLOCK:(f + 1) * BLOCK, :] = blocks_ref[f]
        stacked[(FAN + f) * BLOCK:(FAN + f + 1) * BLOCK, :] = blocks_ref[f]
    signs[...] = (2 * sign_ref[...] - 1).astype(F32)

    def terms(i, p):
        if p == 0:
            own_copies[i].wait()
        from_partner[i, p].wait_recv()
        from_x[i, p] = along_shards(i, p)

    def sketch(i):
        for p in range(CUTS):
            for copy in from_x[i, p]:
                copy.wait_recv()
            lay_out(lambda xx: rx.at[i, xx], p)
        project(own_low(i))
        finish(i)
        spread(i)

    def raw_sketch(i):
        own_copies[i].wait()
        for p in range(CUTS):
            for copy in from_x[i, p]:
                copy.wait_recv()
            lay_out(lambda xx: raw.at[i, xx, 1 - t], p)
        project(low_out.at[i])
        low_from[i] = remote(low_out.at[i], low_in.at[i], el_r.at[i], other_term)

    def raw_own(i):
        for p in range(CUTS):
            lay_out(lambda xx: raw.at[i, xx, t], p)
        project(own_low(i))

    def raw_finish(i):
        low_from[i].wait_recv()
        own_low(i)[...] = own_low(i)[...] + low_in[i]
        finish(i)
        spread(i)

    steps = {
        "begin": begin, "terms": terms, "sketch": sketch, "raw_sketch": raw_sketch, "raw_own": raw_own, "raw_finish": raw_finish,
        "relay": relay, "hop": hop, "cross": cross, "rows_begin": rows_begin, "rows_send": rows_send,
        "rows_pass": rows_pass, "rows_end": rows_end, "inner": inner,
    }
    for step in ORDER:
        steps[step[0]](*step[1:])

    for kind in range(2):
        wait_pieces(send_sem.at[kind], sent[kind] // (ROWS * SKETCH))


def on_device(partials, index_map, sign_bits, blocks):
    count = NX * NT * PART * ROWS
    piece = (ROWS, SKETCH)
    dma = pltpu.SemaphoreType.DMA
    vmem = pl.BlockSpec(memory_space=pltpu.VMEM)
    sketch, kernel = pl.pallas_call(
        kernel_body,
        out_shape=(
            pltpu.VMEM((PART * ROWS, SKETCH), BF16),
            pltpu.VMEM((NY, NZ, NC, PART * ROWS, count), F32),
        ),
        in_specs=[pl.BlockSpec(memory_space=pltpu.HBM)] * 4,
        out_specs=(vmem, vmem),
        scratch_shapes=[
            pltpu.VMEM(index_map.shape[::-1], jnp.int32),
            pltpu.VMEM((BLOCK, BLOCK), jnp.int32),
            pltpu.VMEM(blocks.shape, BF16),
            pltpu.VMEM((PART, NX) + piece, BF16),
            pltpu.VMEM((PART, NX) + piece, BF16),
            pltpu.VMEM((PART, NX) + piece, BF16),
            pltpu.VMEM((PART, NX) + piece, BF16),
            pltpu.VMEM((PART, NX, NT) + piece, BF16),
            pltpu.VMEM((NZ, NC, NY, PART) + piece, BF16),
            pltpu.VMEM((NX, NT, PART) + piece, BF16),
            pltpu.VMEM((ROWS * BLOCK, BLOCK), F32),
            pltpu.VMEM((ROWS * SB, 2 * FAN * BLOCK), BF16),
            pltpu.VMEM((PART * ROWS * SB, BLOCK), F32),
            pltpu.VMEM((PART, ROWS * SB, BLOCK), F32),
            pltpu.VMEM((PART, ROWS * SB, BLOCK), F32),
            pltpu.VMEM((FAN * SB, BLOCK), BF16),
            pltpu.VMEM((BLOCK, BLOCK), F32),
            pltpu.VMEM((2 * FAN * BLOCK, BLOCK), BF16),
            dma((PART + 3,)), dma((2,)),
            dma((PART, CUTS)), dma((PART, CUTS, 3)), dma((PART,)),
            dma((PART, 2)), dma((PART, 8)), dma((PART,)), dma((PART, 2)), dma((1,)), dma((PART, 2, 2, 4)),
        ],
        compiler_params=pltpu.CompilerParams(
            collective_id=0, has_side_effects=True, vmem_limit_bytes=56 * 2**20
        ),
        cost_estimate=pl.CostEstimate(flops=6 * 10**9, bytes_accessed=6 * 10**6, transcendentals=0),
        name="sketch_kernel",
    )(
        partials.reshape(NX, NT, PART, ROWS, -1),
        index_map.T,
        sign_bits.reshape(BLOCK, BLOCK),
        blocks,
    )
    return sketch, kernel.reshape(NY * NZ * NC, PART * ROWS, count)


def solution(mesh):
    placed = (P("group", "tensor", "shard"), P(), P(), P())
    return jax.shard_map(
        on_device,
        mesh=mesh,
        in_specs=placed,
        out_specs=(P(("group", "shard", "tensor"), None), P(None, ("shard", "tensor"), "group")),
        check_vma=False,
    )
```
